32 devices in a mesh: gx: 16 (over z, x, core), gy: 2 (over y).
Axes of the slice: x: 2, y: 2, z: 4, core: 2. Of those that a mesh axis runs over, the one named last changes fastest.
Arguments:
- conc: float32 [32, 1024, 256], P(None, 'gx', 'gy'), may hold values from -4 to 4
- mobility: float32 [32, 1024, 256], P(None, 'gx', 'gy'), may hold values from 0.3 to 3
- block_x: float32 [32, 1024, 64], P(None, 'gx'), may hold values from -0.75 to 0.75
- spike_x: float32 [32, 1024, 4], P(None, 'gx'), may hold values from -3 to 3
- reduced_x: float32 [32, 64, 64], replicated, may hold values from -0.75 to 0.75
- block_y: float32 [32, 256, 128], P(None, 'gy'), may hold values from -0.5 to 0.5
- spike_y: float32 [32, 256, 4], P(None, 'gy'), may hold values from -3 to 3
- reduced_y: float32 [32, 8, 8], replicated, may hold values from -2 to 2
Outputs:
- conc_next: float32 [32, 1024, 256], P(None, 'gx', 'gy')
The draws below stay inside these ranges and needn't reach their ends.
All inputs are finite; a program needn't handle non-finite values.
Results may differ from the reference program's by a relative error of at most 0.00012.
Values sent between devices are 32-bit elements; how exact they have to be, the bound alone decides.
A program may use at most 64 MiB of HBM per device.

```python
import math
import jax
import jax.numpy as jnp
from jax import lax

NZ = 32
CX = 64
CY = 128
NX = 1024
NY = 256
RX = 64
RY = 8


def steps_of(key, shape, split, least, high):
    level, own = 1.0, jax.random.fold_in(key, 6)
    for axis_at, parts in split:
        heights = jnp.exp(jax.random.uniform(jax.random.fold_in(own, axis_at), (parts,), jnp.float32, least / len(split), high / len(split)))
        level = level * jnp.repeat(heights, shape[axis_at] // parts).reshape([-1 if axis == axis_at else 1 for axis in range(len(shape))])
    return level


def normal_values(stream_key, dims, deviation, bound, cuts=(), held_as=jnp.bfloat16):
    level = steps_of(stream_key, dims, cuts, -0.22, 0.18) if cuts else 1.0
    result = jax.random.normal(stream_key, dims, jnp.float32) * deviation * level
    return jnp.minimum(jnp.maximum(result, -bound), bound).astype(held_as)


def setup_inputs(seed: int = 0) -> dict:
    seeds = jax.random.split(jax.random.key(seed), 9)
    conc = normal_values(seeds[0], (NZ, NX, NY), 0.7, 4.0, ((1, 16), (2, 2)), jnp.float32)
    mobility = jnp.clip(jnp.exp(math.log(3.0) - 2.3025851 * jax.random.uniform(seeds[1], (NZ, NX, NY), jnp.float32) ** steps_of(seeds[1], (NZ, NX, NY), ((1, 16), (2, 2)), -0.2, 0.2)), 0.3, 3.0)
    block_x = normal_values(seeds[2], (NZ, NX, CX), CX ** -0.5, 0.75, ((1, 16),), jnp.float32)
    spike_x = normal_values(seeds[3], (NZ, NX, 4), 0.5, 3.0, ((1, 16),), jnp.float32)
    reduced_x = normal_values(seeds[4], (NZ, RX, RX), RX ** -0.5, 0.75, (), jnp.float32)
    block_y = normal_values(seeds[5], (NZ, NY, CY), CY ** -0.5, 0.5, ((1, 2),), jnp.float32)
    spike_y = normal_values(seeds[6], (NZ, NY, 4), 0.5, 3.0, ((1, 2),), jnp.float32)
    reduced_y = normal_values(seeds[7], (NZ, RY, RY), RY ** -0.5, 2.0, (), jnp.float32)
    return {"conc": conc, "mobility": mobility, "block_x": block_x, "spike_x": spike_x, "reduced_x": reduced_x, "block_y": block_y, "spike_y": spike_y, "reduced_y": reduced_y}


HIGH = lax.Precision.HIGHEST


def explicit_part(conc, mobility):
    def roll_sum(field):
        return (jnp.roll(field, 1, 1) + jnp.roll(field, -1, 1)
                + jnp.roll(field, 1, 2) + jnp.roll(field, -1, 2))
    lap = roll_sum(conc) - 4.0 * conc
    mu = conc * conc * conc - conc - 1.0 * lap
    sq = conc * conc
    mob = mobility * (0.25 + sq) / (1.0 + sq)
    div = jnp.zeros_like(conc)
    for shift, axis in ((1, 1), (-1, 1), (1, 2), (-1, 2)):
        div = div + 0.5 * (jnp.roll(mob, shift, axis) + mob) * (jnp.roll(mu, shift, axis) - mu)
    return conc + 0.02 * div


def solve_lines_x(field, block_x, spike_x, reduced_x):
    planes, total, cols = field.shape
    width = block_x.shape[2]
    count = total // width
    mats = block_x.reshape(planes, count, width, width)
    lin = jnp.einsum('zpij,zpjn->zpin', mats, field.reshape(planes, count, width, cols), precision=HIGH)
    rims = jnp.concatenate([lin[:, :, 0:2], lin[:, :, width - 2:]], axis=2).reshape(planes, 4 * count, cols)
    unknowns = jnp.einsum('zrk,zkn->zrn', reduced_x, rims, precision=HIGH).reshape(planes, count, 4, cols)
    coupled = jnp.concatenate([jnp.roll(unknowns, 1, 1)[:, :, 2:4], jnp.roll(unknowns, -1, 1)[:, :, 0:2]], axis=2)
    spikes = spike_x.reshape(planes, count, width, 4)
    out = lin - jnp.einsum('zpik,zpkn->zpin', spikes, coupled, precision=HIGH)
    return out.reshape(planes, total, cols)


def solve_lines_y(field, block_y, spike_y, reduced_y):
    planes, rows, total = field.shape
    width = block_y.shape[2]
    count = total // width
    mats = block_y.reshape(planes, count, width, width)
    lin = jnp.einsum('zqij,zxqj->zxqi', mats, field.reshape(planes, rows, count, width), precision=HIGH)
    rims = jnp.concatenate([lin[..., 0:2], lin[..., width - 2:]], axis=3).reshape(planes, rows, 4 * count)
    unknowns = jnp.einsum('zrk,zxk->zxr', reduced_y, rims, precision=HIGH).reshape(planes, rows, count, 4)
    coupled = jnp.concatenate([jnp.roll(unknowns, 1, 2)[..., 2:4], jnp.roll(unknowns, -1, 2)[..., 0:2]], axis=3)
    spikes = spike_y.reshape(planes, count, width, 4)
    out = lin - jnp.einsum('zqik,zxqk->zxqi', spikes, coupled, precision=HIGH)
    return out.reshape(planes, rows, total)


def reference(conc, mobility, block_x, spike_x, reduced_x, block_y, spike_y, reduced_y):
    rhs = explicit_part(conc, mobility)
    xsol = solve_lines_x(rhs, block_x, spike_x, reduced_x)
    return solve_lines_y(xsol, block_y, spike_y, reduced_y)
```

```python
import functools
import jax
import jax.numpy as jnp
from jax import lax
from jax.experimental import pallas as pl
from jax.experimental.pallas import tpu as pltpu
from jax.sharding import PartitionSpec as P

F32 = jnp.float32
BF16 = jnp.bfloat16
MESH = pl.DeviceIdType.MESH
HIGH = lax.Precision.HIGHEST


def split(value):
    hi = value.astype(BF16)
    lo = (value - hi.astype(F32)).astype(BF16)
    return hi, lo


def iota(shape, axis):
    return lax.broadcasted_iota(jnp.int32, shape, axis)


def mobile(prefactor, centre):
    sq = centre * centre
    return prefactor * (0.25 + sq) / (1.0 + sq)


def picks(place, j, whole):
    pick = 4 * place + jnp.where(j < 2, j - 2, j + 2)
    pick = jnp.where(pick < 0, pick + whole, pick)
    return jnp.where(pick >= whole, pick - whole, pick)


def kernel(
    n, m,
    conc_h, mob_h, bx_h, sx_h, rx_h, by_h, sy_h, ry_h, out_h,
    c_ref, b_ref, bx, sx, rx, by, sy, ry, out,
    xs_dn, xs_up, xr_dn, xr_up, ys, yr, cr,
    mux, mobx, mus, mobs, cs,
    bxc, byc, xl, yfull, rims, rrecv, recm, wsend, wrecv, sxp, yrims, ryc,
    load_sem, out_sem, xsem_s, xsem_r, ysem_s, ysem_r, csem_s, csem_r,
    a_s, a_r, w_s, w_r, g_s, g_r,
):
    NZ, X, Y = c_ref.shape
    owned = NZ // n
    R = 4 * n
    shift_owned = (4 * owned).bit_length() - 1
    i = lax.axis_index("gx")
    j = lax.axis_index("gy")
    up, dn = lax.rem(i + 1, n), lax.rem(i + n - 1, n)
    hi, lo = lax.rem(j + 1, m), lax.rem(j + m - 1, m)
    sides = (hi,) if m == 2 else (lo, hi)

    loads = [
        pltpu.make_async_copy(src, dst, load_sem.at[k])
        for k, (src, dst) in enumerate((
            (conc_h, c_ref), (mob_h, b_ref), (bx_h, bx), (sx_h, sx),
            (rx_h.at[pl.ds(i * owned, owned)], rx), (by_h, by), (sy_h, sy), (ry_h, ry),
        ))
    ]
    for load in loads:
        load.start()

    barrier = pltpu.get_barrier_semaphore()
    peers = [(lax.rem(i + t, n), j) for t in range(1, n)]
    peers += [(i, lax.rem(j + t, m)) for t in range(1, m)]
    peers += [(a, b) for a in (dn, up) for b in sides]
    for peer in peers:
        pl.semaphore_signal(barrier, inc=1, device_id=peer, device_id_type=MESH)

    loads[0].wait()
    loads[1].wait()
    xs_dn[0] = c_ref[:, 0, :]
    xs_dn[1] = c_ref[:, 1, :]
    xs_dn[2] = b_ref[:, 0, :]
    xs_up[0] = c_ref[:, X - 2, :]
    xs_up[1] = c_ref[:, X - 1, :]
    xs_up[2] = b_ref[:, X - 1, :]
    lane = iota((X, Y), 1)
    row = iota((X, Y), 0)
    group = lane >> 2
    pc = jnp.zeros((X, Y), F32)
    pb = jnp.zeros((X, Y), F32)
    for z in range(NZ):
        mine = group == z
        pc = jnp.where(mine, pltpu.roll(c_ref[z], (4 * z + 2) % Y, 1), pc)
        pb = jnp.where(mine, pltpu.roll(b_ref[z], (4 * z + 2) % Y, 1), pb)
    ys[0] = pc
    ys[1] = pb

    pl.semaphore_wait(barrier, len(peers))

    def remote(src, dst, ssem, rsem, who):
        return pltpu.make_async_remote_copy(
            src_ref=src, dst_ref=dst, send_sem=ssem, recv_sem=rsem,
            device_id=who, device_id_type=MESH)

    halo = [
        remote(xs_dn, xr_up, xsem_s.at[0], xsem_r.at[0], (dn, j)),
        remote(xs_up, xr_dn, xsem_s.at[1], xsem_r.at[1], (up, j)),
    ]
    for k, side in enumerate(sides):
        slot = k if m == 2 else 1 - k
        halo.append(remote(ys, yr.at[slot], ysem_s.at[k], ysem_r.at[k], (i, side)))
        halo.append(remote(ys.at[0, 0:8], cr.at[1, slot], csem_s.at[0, k], csem_r.at[0, k], (dn, side)))
        halo.append(remote(ys.at[0, X - 8:X], cr.at[0, slot], csem_s.at[1, k], csem_r.at[1, k], (up, side)))
    for copy in halo:
        copy.start()

    loads[2].wait()

    def prep_x(z, carry):
        h, l = split(bx[z])
        h32 = h.astype(F32)
        bxc[z, :, 0:2 * X] = jnp.concatenate([h32, h32], axis=1).astype(BF16)
        bxc[z, :, 2 * X:3 * X] = l
        return carry

    lax.fori_loop(0, NZ, prep_x, 0, unroll=4)

    for copy in halo:
        copy.wait_recv()

    lo_slot, hi_slot = (0, 0) if m == 2 else (0, 1)
    k4 = lane & 3
    low = k4 < 2
    pc = ys[0]
    ec = jnp.where(low, yr[lo_slot, 0], yr[hi_slot, 0])
    eb = jnp.where(low, yr[lo_slot, 1], yr[hi_slot, 1])
    low1 = low[0:1]
    cd = jnp.where(low1, cr[0, lo_slot, 7:8, :], cr[0, hi_slot, 7:8, :])
    cu = jnp.where(low1, cr[1, lo_slot, 0:1, :], cr[1, hi_slot, 0:1, :])
    fwd = lambda a: pltpu.roll(a, 1, 1)
    bwd = lambda a: pltpu.roll(a, Y - 1, 1)
    sum_y = jnp.where(low, fwd(ec) + bwd(pc), bwd(ec) + fwd(pc))
    sum_x = (jnp.where(row == 0, cd, pltpu.roll(ec, 1, 0))
             + jnp.where(row == X - 1, cu, pltpu.roll(ec, X - 1, 0)))
    emu = ec * ec * ec - ec - (sum_x + sum_y - 4.0 * ec)
    emob = mobile(eb, ec)
    swap = lambda a: jnp.where(k4 == 1, bwd(a), fwd(a))
    cs[...] = swap(ec)
    mus[...] = swap(emu)
    mobs[...] = swap(emob)

    zlane = iota((NZ, Y), 1)
    zrow = iota((NZ, Y), 0)
    for s, (near, far, own, corner) in enumerate((
        (xr_dn[1], xr_dn[0], xs_dn[0], cd),
        (xr_up[0], xr_up[1], xs_up[1], cu),
    )):
        c_lo = jnp.sum(jnp.where(zlane == 4 * zrow + 1, corner, 0.0), axis=1, keepdims=True)
        c_hi = jnp.sum(jnp.where(zlane == 4 * zrow + 2, corner, 0.0), axis=1, keepdims=True)
        side_lo = jnp.where(zlane == 0, c_lo, fwd(near))
        side_hi = jnp.where(zlane == Y - 1, c_hi, bwd(near))
        mux[s] = near * near * near - near - (far + own + side_lo + side_hi - 4.0 * near)
        mobx[s] = mobile((xr_dn if s == 0 else xr_up)[2], near)

    def plane_x(q, zz):
        z = q * owned + zz
        c = c_ref[z]
        unpack = Y - 2 - 4 * z
        cy = pltpu.roll(cs[...], unpack, 1)
        c_ym = jnp.where(lane == 0, cy, fwd(c))
        c_yp = jnp.where(lane == Y - 1, cy, bwd(c))
        c_xm = jnp.where(row == 0, xr_dn[1, pl.ds(z, 1), :], pltpu.roll(c, 1, 0))
        c_xp = jnp.where(row == X - 1, xr_up[0, pl.ds(z, 1), :], pltpu.roll(c, X - 1, 0))
        mu = c * c * c - c - (c_xm + c_xp + c_ym + c_yp - 4.0 * c)
        mob = mobile(b_ref[z], c)
        muy = pltpu.roll(mus[...], unpack, 1)
        moby = pltpu.roll(mobs[...], unpack, 1)
        fy = (jnp.where(lane == Y - 1, moby, bwd(mob)) + mob) * (jnp.where(lane == Y - 1, muy, bwd(mu)) - mu)
        fy_m = jnp.where(lane == 0, (mob + moby) * (mu - muy), fwd(fy))
        mu_dn, mu_up = mux[0, pl.ds(z, 1), :], mux[1, pl.ds(z, 1), :]
        mob_dn, mob_up = mobx[0, pl.ds(z, 1), :], mobx[1, pl.ds(z, 1), :]
        fx = ((jnp.where(row == X - 1, mob_up, pltpu.roll(mob, X - 1, 0)) + mob)
              * (jnp.where(row == X - 1, mu_up, pltpu.roll(mu, X - 1, 0)) - mu))
        fx_m = jnp.where(row == 0, (mob + mob_dn) * (mu - mu_dn), pltpu.roll(fx, 1, 0))
        rhs = c + 0.01 * ((fy - fy_m) + (fx - fx_m))
        rh, rl = split(rhs)
        lin = jnp.dot(bxc[z], jnp.concatenate([rh, rl, rh], axis=0), preferred_element_type=F32)
        xl[z] = lin
        rims[q, 4 * zz:4 * zz + 2, :] = lin[0:2]
        rims[q, 4 * zz + 2:4 * zz + 4, :] = lin[X - 2:X]

    def rim_copy(t):
        who = lax.rem(i + 1 + t, n)
        return remote(rims.at[who], rrecv.at[i], a_s.at[t], a_r.at[t], (who, j))

    def step_x(t, carry):
        who = lax.rem(i + 1 + t, n)
        for zz in range(owned):
            plane_x(who, zz)
        rim_copy(t).start()
        return carry

    lax.fori_loop(0, n - 1, step_x, 0)
    for zz in range(owned):
        plane_x(i, zz)
    rrecv[i] = rims[i]

    loads[4].wait()
    M = NZ * 4
    def parts_of(index):
        return index >> shift_owned, (index >> 2) & (owned - 1), index & 3
    bp, bz, bk = parts_of(iota((R, M), 1))
    ap, az, ak = parts_of(iota((M, R), 0))
    wanted = picks(ap, ak, R) == iota((M, R), 1)
    source = (4 * bp + bk) == iota((R, M), 0)
    big_h = jnp.zeros((M, M), F32)
    big_l = jnp.zeros((M, M), F32)
    for zz in range(owned):
        left = jnp.where(wanted & (az == zz), 1.0, 0.0).astype(BF16)
        right = jnp.where(source & (bz == zz), 1.0, 0.0).astype(BF16)
        rh, rl = split(rx[zz])
        for part, add in ((rh, 0), (rl, 1)):
            chosen = jnp.dot(left, part, preferred_element_type=F32).astype(BF16)
            moved = jnp.dot(chosen, right, preferred_element_type=F32)
            if add == 0:
                big_h = big_h + moved
            else:
                big_l = big_l + moved
    recm[:, 0:M] = big_h.astype(BF16)
    recm[:, M:2 * M] = big_h.astype(BF16)
    recm[:, 2 * M:3 * M] = big_l.astype(BF16)

    for k in (3, 5, 6, 7):
        loads[k].wait()

    def prep_y(z, carry):
        h, l = split(by[z])
        byc[z, :, 0:Y] = h
        byc[z, :, Y:2 * Y] = h
        byc[z, :, 2 * Y:3 * Y] = l
        return carry

    lax.fori_loop(0, NZ, prep_y, 0, unroll=4)

    flat = jnp.concatenate([sx[z] for z in range(NZ)], axis=0)
    sxp[...] = jnp.transpose(flat, (1, 0))

    spread_z = iota((NZ, Y), 0)
    spread_l = iota((NZ, Y), 1)
    coeff = jnp.zeros((4 * m, Y), F32)
    for jj in range(4):
        off = jj - 2 if jj < 2 else jj + 2
        pick = lax.rem(4 * j + off + 4 * m, 4 * m)
        spread = jnp.where(spread_l == 4 * spread_z + jj, 1.0, 0.0)
        coeff = coeff + jnp.dot(ry[pick], spread, precision=HIGH, preferred_element_type=F32)
    ryc[...] = coeff

    for t in range(n - 1):
        rim_copy(t).wait_recv()
    vh, vl = split(rrecv[...].reshape(M, Y))
    w = jnp.dot(recm[...], jnp.concatenate([vh, vl, vh], axis=0), preferred_element_type=F32)
    wsend[...] = w.reshape(n, 4 * owned, Y)

    def w_copy(t):
        who = lax.rem(i + 1 + t, n)
        return remote(wsend.at[who], wrecv.at[i], w_s.at[t], w_r.at[t], (who, j))

    for t in range(n - 1):
        w_copy(t).start()
    wrecv[i] = wsend[i]

    def plane_y(q, zz, packed):
        z = q * owned + zz
        w = wrecv[q]
        spikes = pltpu.roll(sxp[...], lax.rem(Y - 4 * z, Y), 1)
        xsol = xl[z]
        for k in range(4):
            xsol = xsol - spikes[:, k:k + 1] * w[4 * zz + k:4 * zz + k + 1, :]
        xh, xlow = split(xsol)
        lin = lax.dot_general(
            jnp.concatenate([xh, xlow, xh], axis=1), byc[z],
            (((1,), (1,)), ((), ())), preferred_element_type=F32)
        yfull[z] = lin
        return jnp.where(group == z, pltpu.roll(lin, lax.rem(4 * z + 2, Y), 1), packed)

    packed = jnp.zeros((X, Y), F32)
    for zz in range(owned):
        packed = plane_y(i, zz, packed)

    def step_y(t, packed):
        w_copy(t).wait_recv()
        who = lax.rem(i + n - 1 - t, n)
        for zz in range(owned):
            packed = plane_y(who, zz, packed)
        return packed

    packed = lax.fori_loop(0, n - 1, step_y, packed)
    yrims[j] = jnp.where(low, pltpu.roll(packed, Y - 2, 1), pltpu.roll(packed, 2, 1))

    def g_copy(t):
        who = lax.rem(j + 1 + t, m)
        return remote(yrims.at[j], yrims.at[j], g_s.at[t], g_r.at[t], (i, who))

    for t in range(m - 1):
        g_copy(t).start()
    for t in range(m - 1):
        g_copy(t).wait_recv()

    total = jnp.zeros((X, Y), F32)
    klane = iota((1, Y), 1) & 3
    for g in range(m):
        field = yrims[g]
        for d in range(-3, 4):
            factor = jnp.zeros((1, Y), F32)
            for jj in range(4):
                if 0 <= jj - d < 4:
                    factor = jnp.where(klane == jj, ryc[4 * g + jj - d:4 * g + jj - d + 1, :], factor)
            total = total + factor * (field if d == 0 else pltpu.roll(field, d % Y, 1))
    cs[...] = total

    def finish(z, carry):
        mine = pltpu.roll(cs[...], lax.rem(Y - 4 * z, Y), 1)
        spikes = sy[z]
        value = yfull[z]
        for k in range(4):
            value = value - mine[:, k:k + 1] * spikes[k:k + 1, :]
        out[z] = value
        return carry

    chunks = 4
    size = NZ // chunks
    stores = []
    for k in range(chunks):
        lax.fori_loop(k * size, (k + 1) * size, finish, 0, unroll=2)
        store = pltpu.make_async_copy(
            out.at[pl.ds(k * size, size)], out_h.at[pl.ds(k * size, size)], out_sem.at[k])
        store.start()
        stores.append(store)
    for copy in halo:
        copy.wait_send()
    for t in range(n - 1):
        rim_copy(t).wait_send()
        w_copy(t).wait_send()
    for t in range(m - 1):
        g_copy(t).wait_send()
    for store in stores:
        store.wait()


def body(conc, mobility, block_x, spike_x, reduced_x, block_y, spike_y, reduced_y):
    n, m = lax.axis_size("gx"), lax.axis_size("gy")
    NZ, X, Y = conc.shape
    owned = NZ // n
    M = 4 * NZ
    nside = 1 if m == 2 else 2
    vm = lambda *shape: pltpu.VMEM(shape, F32)
    vb = lambda *shape: pltpu.VMEM(shape, BF16)
    dma = lambda *shape: pltpu.SemaphoreType.DMA(shape)
    sxt = jnp.transpose(spike_x, (0, 2, 1))
    syt = jnp.transpose(spike_y, (0, 2, 1))
    ryt = jnp.transpose(reduced_y, (1, 2, 0))
    scratch = [
        vm(NZ, X, Y), vm(NZ, X, Y), vm(NZ, X, X), vm(NZ, 4, X), vm(owned, 4 * n, 4 * n),
        vm(NZ, Y, Y), vm(NZ, 4, Y), vm(4 * m, 4 * m, NZ), vm(NZ, X, Y),
        vm(3, NZ, Y), vm(3, NZ, Y), vm(3, NZ, Y), vm(3, NZ, Y),
        vm(2, X, Y), vm(nside, 2, X, Y), vm(2, nside, 8, Y),
        vm(2, NZ, Y), vm(2, NZ, Y), vm(X, Y), vm(X, Y), vm(X, Y),
        vb(NZ, X, 3 * X), vb(NZ, Y, 3 * Y), vm(NZ, X, Y), vm(NZ, X, Y),
        vm(n, 4 * owned, Y), vm(n, 4 * owned, Y), vb(M, 3 * M),
        vm(n, 4 * owned, Y), vm(n, 4 * owned, Y), vm(X, M), vm(m, X, Y), vm(4 * m, Y),
        dma(8), dma(4), dma(2), dma(2), dma(nside), dma(nside), dma(2, nside), dma(2, nside),
        dma(n - 1), dma(n - 1), dma(n - 1), dma(n - 1), dma(m - 1), dma(m - 1),
    ]
    return pl.pallas_call(
        functools.partial(kernel, n, m),
        out_shape=jax.ShapeDtypeStruct(conc.shape, F32),
        in_specs=[pl.BlockSpec(memory_space=pl.ANY)] * 8,
        out_specs=pl.BlockSpec(memory_space=pl.ANY),
        scratch_shapes=scratch,
        compiler_params=pltpu.CompilerParams(
            collective_id=0, has_side_effects=True, vmem_limit_bytes=40 * 2**20),
        cost_estimate=pl.CostEstimate(flops=10**9, bytes_accessed=8 * 2**20, transcendentals=0),
    )(conc, mobility, block_x, sxt, reduced_x, block_y, syt, ryt)


def solution(mesh):
    in_specs = (
        P(None, "gx", "gy"),
        P(None, "gx", "gy"),
        P(None, "gx", None),
        P(None, "gx", None),
        P(),
        P(None, "gy", None),
        P(None, "gy", None),
        P(),
    )
    out_specs = P(None, "gx", "gy")
    return jax.shard_map(body, mesh=mesh, in_specs=in_specs, out_specs=out_specs, check_vma=False)
```

```python
import functools
import jax
import jax.numpy as jnp
from jax import lax
from jax.experimental import pallas as pl
from jax.experimental.pallas import tpu as pltpu
from jax.sharding import PartitionSpec as P

F32 = jnp.float32
BF16 = jnp.bfloat16
MESH = pl.DeviceIdType.MESH
HIGH = lax.Precision.HIGHEST


def split(value):
    hi = value.astype(BF16)
    lo = (value - hi.astype(F32)).astype(BF16)
    return hi, lo


def iota(shape, axis):
    return lax.broadcasted_iota(jnp.int32, shape, axis)


def mobile(prefactor, centre):
    sq = centre * centre
    return prefactor * (0.25 + sq) / (1.0 + sq)


def picks(place, j, whole):
    pick = 4 * place + jnp.where(j < 2, j - 2, j + 2)
    pick = jnp.where(pick < 0, pick + whole, pick)
    return jnp.where(pick >= whole, pick - whole, pick)


def kernel(
    n, m,
    conc_h, mob_h, bx_h, sx_h, rx_h, by_h, sy_h, ry_h, out_h,
    c_ref, b_ref, bx, sx, rx, by, sy, ry, out,
    xs_dn, xs_up, xr_dn, xr_up, ys, yr, cr,
    mux, mobx, mus, mobs, cs,
    bxc, byc, xl, yfull, rims, rrecv, recm, wsend, wrecv, sxp, yrims, ryc,
    mu_ref, sumx, sumy, sxb,
    load_sem, out_sem, xsem_s, xsem_r, ysem_s, ysem_r, csem_s, csem_r,
    a_s, a_r, w_s, w_r, g_s, g_r,
):
    NZ, X, Y = c_ref.shape
    owned = NZ // n
    R = 4 * n
    shift_owned = (4 * owned).bit_length() - 1
    i = lax.axis_index("gx")
    j = lax.axis_index("gy")
    up, dn = lax.rem(i + 1, n), lax.rem(i + n - 1, n)
    hi, lo = lax.rem(j + 1, m), lax.rem(j + m - 1, m)
    sides = (hi,) if m == 2 else (lo, hi)

    loads = [
        pltpu.make_async_copy(src, dst, load_sem.at[k])
        for k, (src, dst) in enumerate((
            (conc_h, c_ref), (mob_h, b_ref), (bx_h, bx), (sx_h, sx),
            (rx_h.at[pl.ds(i * owned, owned)], rx), (by_h, by), (sy_h, sy), (ry_h, ry),
        ))
    ]
    for load in loads:
        load.start()

    barrier = pltpu.get_barrier_semaphore()
    peers = [(lax.rem(i + t, n), j) for t in range(1, n)]
    peers += [(i, lax.rem(j + t, m)) for t in range(1, m)]
    peers += [(a, b) for a in (dn, up) for b in sides]
    for peer in peers:
        pl.semaphore_signal(barrier, inc=1, device_id=peer, device_id_type=MESH)

    loads[0].wait()
    loads[1].wait()
    xs_dn[0] = c_ref[:, 0, :]
    xs_dn[1] = c_ref[:, 1, :]
    xs_dn[2] = b_ref[:, 0, :]
    xs_up[0] = c_ref[:, X - 2, :]
    xs_up[1] = c_ref[:, X - 1, :]
    xs_up[2] = b_ref[:, X - 1, :]
    lane = iota((X, Y), 1)
    row = iota((X, Y), 0)
    group = lane >> 2
    pc = jnp.zeros((X, Y), F32)
    pb = jnp.zeros((X, Y), F32)
    for z in range(NZ):
        mine = group == z
        pc = jnp.where(mine, pltpu.roll(c_ref[z], (4 * z + 2) % Y, 1), pc)
        pb = jnp.where(mine, pltpu.roll(b_ref[z], (4 * z + 2) % Y, 1), pb)
    ys[0] = pc
    ys[1] = pb

    pl.semaphore_wait(barrier, len(peers))

    def remote(src, dst, ssem, rsem, who):
        return pltpu.make_async_remote_copy(
            src_ref=src, dst_ref=dst, send_sem=ssem, recv_sem=rsem,
            device_id=who, device_id_type=MESH)

    halo = [
        remote(xs_dn, xr_up, xsem_s.at[0], xsem_r.at[0], (dn, j)),
        remote(xs_up, xr_dn, xsem_s.at[1], xsem_r.at[1], (up, j)),
    ]
    for k, side in enumerate(sides):
        slot = k if m == 2 else 1 - k
        halo.append(remote(ys, yr.at[slot], ysem_s.at[k], ysem_r.at[k], (i, side)))
        halo.append(remote(ys.at[0, 0:8], cr.at[1, slot], csem_s.at[0, k], csem_r.at[0, k], (dn, side)))
        halo.append(remote(ys.at[0, X - 8:X], cr.at[0, slot], csem_s.at[1, k], csem_r.at[1, k], (up, side)))
    for copy in halo:
        copy.start()

    loads[2].wait()

    def prep_x(z, carry):
        h, l = split(bx[z])
        h32 = h.astype(F32)
        bxc[z, :, 0:2 * X] = jnp.concatenate([h32, h32], axis=1).astype(BF16)
        bxc[z, :, 2 * X:3 * X] = l
        return carry

    lax.fori_loop(0, NZ, prep_x, 0, unroll=4)

    fwd = lambda a: pltpu.roll(a, 1, 1)
    bwd = lambda a: pltpu.roll(a, Y - 1, 1)

    def prep_mu(z, carry):
        c = c_ref[z]
        around = (jnp.where(lane == 0, 0.0, fwd(c)) + jnp.where(lane == Y - 1, 0.0, bwd(c))
                  + jnp.where(row == 0, 0.0, pltpu.roll(c, 1, 0))
                  + jnp.where(row == X - 1, 0.0, pltpu.roll(c, X - 1, 0)))
        mu_ref[z] = c * c * c - c - (around - 4.0 * c)
        mob = mobile(b_ref[z], c)
        b_ref[z] = mob
        sumx[z] = mob + pltpu.roll(mob, X - 1, 0)
        sumy[z] = mob + bwd(mob)
        return carry

    lax.fori_loop(0, NZ, prep_mu, 0, unroll=4)

    for copy in halo:
        copy.wait_recv()

    mu_ref[:, 0, :] = mu_ref[:, 0, :] - xr_dn[1]
    mu_ref[:, X - 1, :] = mu_ref[:, X - 1, :] - xr_up[0]

    lo_slot, hi_slot = (0, 0) if m == 2 else (0, 1)
    k4 = lane & 3
    low = k4 < 2
    pc = ys[0]
    ec = jnp.where(low, yr[lo_slot, 0], yr[hi_slot, 0])
    eb = jnp.where(low, yr[lo_slot, 1], yr[hi_slot, 1])
    low1 = low[0:1]
    cd = jnp.where(low1, cr[0, lo_slot, 7:8, :], cr[0, hi_slot, 7:8, :])
    cu = jnp.where(low1, cr[1, lo_slot, 0:1, :], cr[1, hi_slot, 0:1, :])
    sum_y = jnp.where(low, fwd(ec) + bwd(pc), bwd(ec) + fwd(pc))
    sum_x = (jnp.where(row == 0, cd, pltpu.roll(ec, 1, 0))
             + jnp.where(row == X - 1, cu, pltpu.roll(ec, X - 1, 0)))
    emu = ec * ec * ec - ec - (sum_x + sum_y - 4.0 * ec)
    emob = mobile(eb, ec)
    swap = lambda a: jnp.where(k4 == 1, bwd(a), fwd(a))
    cs[...] = swap(ec)
    mus[...] = swap(emu)
    mobs[...] = swap(emob)

    zlane = iota((NZ, Y), 1)
    zrow = iota((NZ, Y), 0)
    for s, (near, far, own, corner) in enumerate((
        (xr_dn[1], xr_dn[0], xs_dn[0], cd),
        (xr_up[0], xr_up[1], xs_up[1], cu),
    )):
        c_lo = jnp.sum(jnp.where(zlane == 4 * zrow + 1, corner, 0.0), axis=1, keepdims=True)
        c_hi = jnp.sum(jnp.where(zlane == 4 * zrow + 2, corner, 0.0), axis=1, keepdims=True)
        side_lo = jnp.where(zlane == 0, c_lo, fwd(near))
        side_hi = jnp.where(zlane == Y - 1, c_hi, bwd(near))
        mux[s] = near * near * near - near - (far + own + side_lo + side_hi - 4.0 * near)
        mobx[s] = mobile((xr_dn if s == 0 else xr_up)[2], near)

    edge_y = (lane == 0) | (lane == Y - 1)
    first_y, last_y, first_x, last_x = lane == 0, lane == Y - 1, row == 0, row == X - 1

    def plane_x(q, zz):
        z = q * owned + zz
        unpack = Y - 2 - 4 * z
        mob = b_ref[z]
        mu = mu_ref[z] - jnp.where(edge_y, pltpu.roll(cs[...], unpack, 1), 0.0)
        muy = pltpu.roll(mus[...], unpack, 1)
        moby = mob + pltpu.roll(mobs[...], unpack, 1)
        fy = jnp.where(last_y, moby, sumy[z]) * (jnp.where(last_y, muy, bwd(mu)) - mu)
        fy_m = jnp.where(first_y, moby * (mu - muy), fwd(fy))
        mu_dn, mu_up = mux[0, pl.ds(z, 1), :], mux[1, pl.ds(z, 1), :]
        mob_dn, mob_up = mobx[0, pl.ds(z, 1), :], mobx[1, pl.ds(z, 1), :]
        fx = (jnp.where(last_x, mob_up + mob, sumx[z])
              * (jnp.where(last_x, mu_up, pltpu.roll(mu, X - 1, 0)) - mu))
        fx_m = jnp.where(first_x, (mob + mob_dn) * (mu - mu_dn), pltpu.roll(fx, 1, 0))
        rhs = c_ref[z] + 0.01 * ((fy - fy_m) + (fx - fx_m))
        rh, rl = split(rhs)
        lin = jnp.dot(bxc[z], jnp.concatenate([rh, rl, rh], axis=0), preferred_element_type=F32)
        xl[z] = lin
        rims[q, 4 * zz:4 * zz + 2, :] = lin[0:2]
        rims[q, 4 * zz + 2:4 * zz + 4, :] = lin[X - 2:X]

    def rim_copy(t):
        who = lax.rem(i + 1 + t, n)
        return remote(rims.at[who], rrecv.at[i], a_s.at[t], a_r.at[t], (who, j))

    owners = max(1, 8 // owned)

    def step_x(b, carry):
        for u in range(owners):
            who = lax.rem(i + 1 + b * owners + u, n)
            for zz in range(owned):
                plane_x(who, zz)
        for u in range(owners):
            t = b * owners + u

            @pl.when(t < n - 1)
            def _():
                rim_copy(t).start()
        return carry

    lax.fori_loop(0, n // owners, step_x, 0)
    rrecv[i] = rims[i]

    loads[4].wait()
    M = NZ * 4
    def parts_of(index):
        return index >> shift_owned, (index >> 2) & (owned - 1), index & 3
    bp, bz, bk = parts_of(iota((R, M), 1))
    ap, az, ak = parts_of(iota((M, R), 0))
    wanted = picks(ap, ak, R) == iota((M, R), 1)
    source = (4 * bp + bk) == iota((R, M), 0)
    big_h = jnp.zeros((M, M), F32)
    big_l = jnp.zeros((M, M), F32)
    for zz in range(owned):
        left = jnp.where(wanted & (az == zz), 1.0, 0.0).astype(BF16)
        right = jnp.where(source & (bz == zz), 1.0, 0.0).astype(BF16)
        rh, rl = split(rx[zz])
        for part, add in ((rh, 0), (rl, 1)):
            chosen = jnp.dot(left, part, preferred_element_type=F32).astype(BF16)
            moved = jnp.dot(chosen, right, preferred_element_type=F32)
            if add == 0:
                big_h = big_h + moved
            else:
                big_l = big_l + moved
    recm[:, 0:M] = big_h.astype(BF16)
    recm[:, M:2 * M] = big_h.astype(BF16)
    recm[:, 2 * M:3 * M] = big_l.astype(BF16)

    for k in (3, 7):
        loads[k].wait()

    flat = jnp.concatenate([sx[z] for z in range(NZ)], axis=0)
    sxp[...] = jnp.transpose(flat, (1, 0))

    def prep_spikes(z, carry):
        spikes = pltpu.roll(sxp[...], lax.rem(Y - 4 * z, Y), 1)
        for k in range(4):
            sxb[z, k] = jnp.broadcast_to(spikes[:, k:k + 1], (X, Y))
        return carry

    lax.fori_loop(0, NZ, prep_spikes, 0, unroll=4)

    spread_z = iota((NZ, Y), 0)
    spread_l = iota((NZ, Y), 1)
    coeff = jnp.zeros((4 * m, Y), F32)
    for jj in range(4):
        off = jj - 2 if jj < 2 else jj + 2
        pick = lax.rem(4 * j + off + 4 * m, 4 * m)
        spread = jnp.where(spread_l == 4 * spread_z + jj, 1.0, 0.0)
        coeff = coeff + jnp.dot(ry[pick], spread, precision=HIGH, preferred_element_type=F32)
    ryc[...] = coeff

    for t in range(n - 1):
        rim_copy(t).wait_recv()
    vh, vl = split(rrecv[...].reshape(M, Y))
    w = jnp.dot(recm[...], jnp.concatenate([vh, vl, vh], axis=0), preferred_element_type=F32)
    wsend[...] = w.reshape(n, 4 * owned, Y)

    def w_copy(t):
        who = lax.rem(i + 1 + t, n)
        return remote(wsend.at[who], wrecv.at[i], w_s.at[t], w_r.at[t], (who, j))

    for t in range(n - 1):
        w_copy(t).start()
    wrecv[i] = wsend[i]

    for k in (5, 6):
        loads[k].wait()

    def prep_y(z, carry):
        h, l = split(by[z])
        byc[z, :, 0:Y] = h
        byc[z, :, Y:2 * Y] = h
        byc[z, :, 2 * Y:3 * Y] = l
        return carry

    lax.fori_loop(0, NZ, prep_y, 0, unroll=4)

    def plane_y(q, zz, packed):
        z = q * owned + zz
        w = wrecv[q]
        xsol = xl[z]
        for k in range(4):
            xsol = xsol - sxb[z, k] * w[4 * zz + k:4 * zz + k + 1, :]
        xh, xlow = split(xsol)
        lin = lax.dot_general(
            jnp.concatenate([xh, xlow, xh], axis=1), byc[z],
            (((1,), (1,)), ((), ())), preferred_element_type=F32)
        yfull[z] = lin
        return jnp.where(group == z, pltpu.roll(lin, lax.rem(4 * z + 2, Y), 1), packed)

    def step_y(b, packed):
        for u in range(owners):
            t = b * owners + u

            @pl.when(t < n - 1)
            def _():
                w_copy(t).wait_recv()
        for u in range(owners):
            who = lax.rem(i + 2 * n - 1 - b * owners - u, n)
            for zz in range(owned):
                packed = plane_y(who, zz, packed)
        return packed

    packed = lax.fori_loop(0, n // owners, step_y, jnp.zeros((X, Y), F32))
    yrims[j] = jnp.where(low, pltpu.roll(packed, Y - 2, 1), pltpu.roll(packed, 2, 1))

    def g_copy(t):
        who = lax.rem(j + 1 + t, m)
        return remote(yrims.at[j], yrims.at[j], g_s.at[t], g_r.at[t], (i, who))

    for t in range(m - 1):
        g_copy(t).start()
    for t in range(m - 1):
        g_copy(t).wait_recv()

    total = jnp.zeros((X, Y), F32)
    klane = iota((1, Y), 1) & 3
    for g in range(m):
        field = yrims[g]
        for d in range(-3, 4):
            factor = jnp.zeros((1, Y), F32)
            for jj in range(4):
                if 0 <= jj - d < 4:
                    factor = jnp.where(klane == jj, ryc[4 * g + jj - d:4 * g + jj - d + 1, :], factor)
            total = total + factor * (field if d == 0 else pltpu.roll(field, d % Y, 1))
    cs[...] = total

    def finish(z, carry):
        mine = pltpu.roll(cs[...], lax.rem(Y - 4 * z, Y), 1)
        spikes = sy[z]
        value = yfull[z]
        for k in range(4):
            value = value - mine[:, k:k + 1] * spikes[k:k + 1, :]
        out[z] = value
        return carry

    chunks = 4
    size = NZ // chunks
    stores = []
    for k in range(chunks):
        lax.fori_loop(k * size, (k + 1) * size, finish, 0, unroll=8)
        store = pltpu.make_async_copy(
            out.at[pl.ds(k * size, size)], out_h.at[pl.ds(k * size, size)], out_sem.at[k])
        store.start()
        stores.append(store)
    for copy in halo:
        copy.wait_send()
    for t in range(n - 1):
        rim_copy(t).wait_send()
        w_copy(t).wait_send()
    for t in range(m - 1):
        g_copy(t).wait_send()
    for store in stores:
        store.wait()


def body(conc, mobility, block_x, spike_x, reduced_x, block_y, spike_y, reduced_y):
    n, m = lax.axis_size("gx"), lax.axis_size("gy")
    NZ, X, Y = conc.shape
    owned = NZ // n
    M = 4 * NZ
    nside = 1 if m == 2 else 2
    vm = lambda *shape: pltpu.VMEM(shape, F32)
    vb = lambda *shape: pltpu.VMEM(shape, BF16)
    dma = lambda *shape: pltpu.SemaphoreType.DMA(shape)
    sxt = jnp.transpose(spike_x, (0, 2, 1))
    syt = jnp.transpose(spike_y, (0, 2, 1))
    ryt = jnp.transpose(reduced_y, (1, 2, 0))
    scratch = [
        vm(NZ, X, Y), vm(NZ, X, Y), vm(NZ, X, X), vm(NZ, 4, X), vm(owned, 4 * n, 4 * n),
        vm(NZ, Y, Y), vm(NZ, 4, Y), vm(4 * m, 4 * m, NZ), vm(NZ, X, Y),
        vm(3, NZ, Y), vm(3, NZ, Y), vm(3, NZ, Y), vm(3, NZ, Y),
        vm(2, X, Y), vm(nside, 2, X, Y), vm(2, nside, 8, Y),
        vm(2, NZ, Y), vm(2, NZ, Y), vm(X, Y), vm(X, Y), vm(X, Y),
        vb(NZ, X, 3 * X), vb(NZ, Y, 3 * Y), vm(NZ, X, Y), vm(NZ, X, Y),
        vm(n, 4 * owned, Y), vm(n, 4 * owned, Y), vb(M, 3 * M),
        vm(n, 4 * owned, Y), vm(n, 4 * owned, Y), vm(X, M), vm(m, X, Y), vm(4 * m, Y),
        vm(NZ, X, Y), vm(NZ, X, Y), vm(NZ, X, Y), vm(NZ, 4, X, Y),
        dma(8), dma(4), dma(2), dma(2), dma(nside), dma(nside), dma(2, nside), dma(2, nside),
        dma(n - 1), dma(n - 1), dma(n - 1), dma(n - 1), dma(m - 1), dma(m - 1),
    ]
    return pl.pallas_call(
        functools.partial(kernel, n, m),
        out_shape=jax.ShapeDtypeStruct(conc.shape, F32),
        in_specs=[pl.BlockSpec(memory_space=pl.ANY)] * 8,
        out_specs=pl.BlockSpec(memory_space=pl.ANY),
        scratch_shapes=scratch,
        compiler_params=pltpu.CompilerParams(
            collective_id=0, has_side_effects=True, vmem_limit_bytes=60 * 2**20),
        cost_estimate=pl.CostEstimate(flops=10**9, bytes_accessed=8 * 2**20, transcendentals=0),
    )(conc, mobility, block_x, sxt, reduced_x, block_y, syt, ryt)


def solution(mesh):
    in_specs = (
        P(None, "gx", "gy"),
        P(None, "gx", "gy"),
        P(None, "gx", None),
        P(None, "gx", None),
        P(),
        P(None, "gy", None),
        P(None, "gy", None),
        P(),
    )
    out_specs = P(None, "gx", "gy")
    return jax.shard_map(body, mesh=mesh, in_specs=in_specs, out_specs=out_specs, check_vma=False)
```

```python
import functools
import jax
import jax.numpy as jnp
from jax import lax
from jax.experimental import pallas as pl
from jax.experimental.pallas import tpu as pltpu
from jax.sharding import PartitionSpec as P

F32 = jnp.float32
BF16 = jnp.bfloat16
MESH = pl.DeviceIdType.MESH
HIGH = lax.Precision.HIGHEST


def split(value):
    hi = value.astype(BF16)
    lo = (value - hi.astype(F32)).astype(BF16)
    return hi, lo


def iota(shape, axis):
    return lax.broadcasted_iota(jnp.int32, shape, axis)


def mobile(prefactor, centre):
    sq = centre * centre
    return prefactor * (0.25 + sq) / (1.0 + sq)


def picks(place, j, whole):
    pick = 4 * place + jnp.where(j < 2, j - 2, j + 2)
    pick = jnp.where(pick < 0, pick + whole, pick)
    return jnp.where(pick >= whole, pick - whole, pick)


def kernel(
    n, m,
    conc_h, mob_h, bx_h, sx_h, rx_h, by_h, ry_h, lin_h, total_h,
    c_ref, b_ref, bx, sx, rx, by, ry,
    xs_dn, xs_up, xr_dn, xr_up, ys, yr, cr,
    mux, mobx, mus, mobs, cs,
    bxc, byc, xl, yfull, rims, rrecv, recm, wsend, wrecv, sxp, yrims, ryc, byr, byr3, sx3, total_v,
    mu_ref, sumx, sumy, sxb,
    load_sem, out_sem, xsem_s, xsem_r, ysem_s, ysem_r, csem_s, csem_r,
    a_s, a_r, w_s, w_r, g_s, g_r,
):
    NZ, X, Y = c_ref.shape
    owned = NZ // n
    R = 4 * n
    shift_owned = (4 * owned).bit_length() - 1
    i = lax.axis_index("gx")
    j = lax.axis_index("gy")
    up, dn = lax.rem(i + 1, n), lax.rem(i + n - 1, n)
    hi, lo = lax.rem(j + 1, m), lax.rem(j + m - 1, m)
    sides = (hi,) if m == 2 else (lo, hi)

    loads = [
        pltpu.make_async_copy(src, dst, load_sem.at[k])
        for k, (src, dst) in enumerate((
            (conc_h, c_ref), (mob_h, b_ref), (bx_h, bx), (sx_h, sx),
            (rx_h.at[pl.ds(i * owned, owned)], rx), (by_h, by), (ry_h, ry),
        ))
    ]
    loads[0].start()
    loads[1].start()

    barrier = pltpu.get_barrier_semaphore()
    peers = [(lax.rem(i + t, n), j) for t in range(1, n)]
    peers += [(i, lax.rem(j + t, m)) for t in range(1, m)]
    peers += [(a, b) for a in (dn, up) for b in sides]
    for peer in peers:
        pl.semaphore_signal(barrier, inc=1, device_id=peer, device_id_type=MESH)

    loads[0].wait()
    loads[1].wait()
    for load in loads[2:]:
        load.start()
    xs_dn[0] = c_ref[:, 0, :]
    xs_dn[1] = c_ref[:, 1, :]
    xs_dn[2] = b_ref[:, 0, :]
    xs_up[0] = c_ref[:, X - 2, :]
    xs_up[1] = c_ref[:, X - 1, :]
    xs_up[2] = b_ref[:, X - 1, :]
    lane = iota((X, Y), 1)
    row = iota((X, Y), 0)
    group = lane >> 2
    pc = jnp.zeros((X, Y), F32)
    pb = jnp.zeros((X, Y), F32)
    for z in range(NZ):
        mine = group == z
        pc = jnp.where(mine, pltpu.roll(c_ref[z], (4 * z + 2) % Y, 1), pc)
        pb = jnp.where(mine, pltpu.roll(b_ref[z], (4 * z + 2) % Y, 1), pb)
    fwd = lambda a: pltpu.roll(a, 1, 1)
    bwd = lambda a: pltpu.roll(a, Y - 1, 1)
    half = X // 2
    kh = iota((half, Y), 1) & 3
    ys[0:X] = pc
    ys[X:X + half] = jnp.where(
        kh == 0, bwd(pb[half:X]), jnp.where(kh == 3, fwd(pb[half:X]), pb[0:half]))

    pl.semaphore_wait(barrier, len(peers))

    def remote(src, dst, ssem, rsem, who):
        return pltpu.make_async_remote_copy(
            src_ref=src, dst_ref=dst, send_sem=ssem, recv_sem=rsem,
            device_id=who, device_id_type=MESH)

    halo = [
        remote(xs_dn, xr_up, xsem_s.at[0], xsem_r.at[0], (dn, j)),
        remote(xs_up, xr_dn, xsem_s.at[1], xsem_r.at[1], (up, j)),
    ]
    for k, side in enumerate(sides):
        slot = k if m == 2 else 1 - k
        halo.append(remote(ys, yr.at[slot], ysem_s.at[k], ysem_r.at[k], (i, side)))
        halo.append(remote(ys.at[0:8], cr.at[1, slot], csem_s.at[0, k], csem_r.at[0, k], (dn, side)))
        halo.append(remote(ys.at[X - 8:X], cr.at[0, slot], csem_s.at[1, k], csem_r.at[1, k], (up, side)))
    for copy in halo:
        copy.start()

    loads[2].wait()

    def prep_x(z, carry):
        h, l = split(bx[z])
        h32 = h.astype(F32)
        bxc[z, :, 0:2 * X] = jnp.concatenate([h32, h32], axis=1).astype(BF16)
        bxc[z, :, 2 * X:3 * X] = l
        return carry

    lax.fori_loop(0, NZ, prep_x, 0, unroll=4)

    def prep_mu(z, carry):
        c = c_ref[z]
        around = (jnp.where(lane == 0, 0.0, fwd(c)) + jnp.where(lane == Y - 1, 0.0, bwd(c))
                  + jnp.where(row == 0, 0.0, pltpu.roll(c, 1, 0))
                  + jnp.where(row == X - 1, 0.0, pltpu.roll(c, X - 1, 0)))
        mu_ref[z] = c * c * c - c - (around - 4.0 * c)
        mob = mobile(b_ref[z], c)
        b_ref[z] = mob
        sumx[z] = mob + pltpu.roll(mob, X - 1, 0)
        sumy[z] = mob + bwd(mob)
        return carry

    lax.fori_loop(0, NZ, prep_mu, 0, unroll=4)

    for copy in halo:
        copy.wait_recv()

    mu_ref[:, 0, :] = mu_ref[:, 0, :] - xr_dn[1]
    mu_ref[:, X - 1, :] = mu_ref[:, X - 1, :] - xr_up[0]

    lo_slot, hi_slot = (0, 0) if m == 2 else (0, 1)
    k4 = lane & 3
    low = k4 < 2
    pc = ys[0:X]
    ec = jnp.where(low, yr[lo_slot, 0:X], yr[hi_slot, 0:X])
    lo_b, hi_b = yr[lo_slot, X:X + half], yr[hi_slot, X:X + half]
    eb = jnp.concatenate([
        jnp.where(kh < 2, lo_b, hi_b),
        jnp.where(kh < 2, fwd(lo_b), bwd(hi_b))], axis=0)
    low1 = low[0:1]
    cd = jnp.where(low1, cr[0, lo_slot, 7:8, :], cr[0, hi_slot, 7:8, :])
    cu = jnp.where(low1, cr[1, lo_slot, 0:1, :], cr[1, hi_slot, 0:1, :])
    sum_y = jnp.where(low, fwd(ec) + bwd(pc), bwd(ec) + fwd(pc))
    sum_x = (jnp.where(row == 0, cd, pltpu.roll(ec, 1, 0))
             + jnp.where(row == X - 1, cu, pltpu.roll(ec, X - 1, 0)))
    emu = ec * ec * ec - ec - (sum_x + sum_y - 4.0 * ec)
    emob = mobile(eb, ec)
    swap = lambda a: jnp.where(k4 == 1, bwd(a), fwd(a))
    cs[...] = swap(ec)
    mus[...] = swap(emu)
    mobs[...] = swap(emob)

    zlane = iota((NZ, Y), 1)
    zrow = iota((NZ, Y), 0)
    for s, (near, far, own, corner) in enumerate((
        (xr_dn[1], xr_dn[0], xs_dn[0], cd),
        (xr_up[0], xr_up[1], xs_up[1], cu),
    )):
        c_lo = jnp.sum(jnp.where(zlane == 4 * zrow + 1, corner, 0.0), axis=1, keepdims=True)
        c_hi = jnp.sum(jnp.where(zlane == 4 * zrow + 2, corner, 0.0), axis=1, keepdims=True)
        side_lo = jnp.where(zlane == 0, c_lo, fwd(near))
        side_hi = jnp.where(zlane == Y - 1, c_hi, bwd(near))
        mux[s] = near * near * near - near - (far + own + side_lo + side_hi - 4.0 * near)
        mobx[s] = mobile((xr_dn if s == 0 else xr_up)[2], near)

    edge_y = (lane == 0) | (lane == Y - 1)
    first_y, last_y, first_x, last_x = lane == 0, lane == Y - 1, row == 0, row == X - 1

    def plane_x(q, zz):
        z = q * owned + zz
        unpack = Y - 2 - 4 * z
        mob = b_ref[z]
        mu = mu_ref[z] - jnp.where(edge_y, pltpu.roll(cs[...], unpack, 1), 0.0)
        muy = pltpu.roll(mus[...], unpack, 1)
        moby = mob + pltpu.roll(mobs[...], unpack, 1)
        fy = jnp.where(last_y, moby, sumy[z]) * (jnp.where(last_y, muy, bwd(mu)) - mu)
        fy_m = jnp.where(first_y, moby * (mu - muy), fwd(fy))
        mu_dn, mu_up = mux[0, pl.ds(z, 1), :], mux[1, pl.ds(z, 1), :]
        mob_dn, mob_up = mobx[0, pl.ds(z, 1), :], mobx[1, pl.ds(z, 1), :]
        fx = (jnp.where(last_x, mob_up + mob, sumx[z])
              * (jnp.where(last_x, mu_up, pltpu.roll(mu, X - 1, 0)) - mu))
        fx_m = jnp.where(first_x, (mob + mob_dn) * (mu - mu_dn), pltpu.roll(fx, 1, 0))
        rhs = c_ref[z] + 0.01 * ((fy - fy_m) + (fx - fx_m))
        rh, rl = split(rhs)
        lin = jnp.dot(bxc[z], jnp.concatenate([rh, rl, rh], axis=0), preferred_element_type=F32)
        xl[z] = lin
        rims[q, 4 * zz:4 * zz + 2, :] = lin[0:2]
        rims[q, 4 * zz + 2:4 * zz + 4, :] = lin[X - 2:X]

    def rim_copy(t):
        who = lax.rem(i + 1 + t, n)
        return remote(rims.at[who], rrecv.at[i], a_s.at[t], a_r.at[t], (who, j))

    owners = max(1, 8 // owned)

    def step_x(b, carry):
        for u in range(owners):
            who = lax.rem(i + 1 + b * owners + u, n)
            for zz in range(owned):
                plane_x(who, zz)
        for u in range(owners):
            t = b * owners + u

            @pl.when(t < n - 1)
            def _():
                rim_copy(t).start()
        return carry

    lax.fori_loop(0, n // owners, step_x, 0)
    rrecv[i] = rims[i]

    loads[4].wait()
    M = NZ * 4
    def parts_of(index):
        return index >> shift_owned, (index >> 2) & (owned - 1), index & 3
    bp, bz, bk = parts_of(iota((R, M), 1))
    ap, az, ak = parts_of(iota((M, R), 0))
    wanted = picks(ap, ak, R) == iota((M, R), 1)
    source = (4 * bp + bk) == iota((R, M), 0)
    big_h = jnp.zeros((M, M), F32)
    big_l = jnp.zeros((M, M), F32)
    for zz in range(owned):
        left = jnp.where(wanted & (az == zz), 1.0, 0.0).astype(BF16)
        right = jnp.where(source & (bz == zz), 1.0, 0.0).astype(BF16)
        rh, rl = split(rx[zz])
        for part, add in ((rh, 0), (rl, 1)):
            chosen = jnp.dot(left, part, preferred_element_type=F32).astype(BF16)
            moved = jnp.dot(chosen, right, preferred_element_type=F32)
            if add == 0:
                big_h = big_h + moved
            else:
                big_l = big_l + moved
    recm[:, 0:M] = big_h.astype(BF16)
    recm[:, M:2 * M] = big_h.astype(BF16)
    recm[:, 2 * M:3 * M] = big_l.astype(BF16)

    loads[5].wait()

    def prep_y(z, carry):
        h, l = split(by[z])
        byc[z, :, 0:Y] = h
        byc[z, :, Y:2 * Y] = h
        byc[z, :, 2 * Y:3 * Y] = l
        return carry

    lax.fori_loop(0, NZ, prep_y, 0, unroll=4)

    def lin_y(z, packed):
        xh, xlow = split(xl[z])
        lin = lax.dot_general(
            jnp.concatenate([xh, xlow, xh], axis=1), byc[z],
            (((1,), (1,)), ((), ())), preferred_element_type=F32)
        yfull[z] = lin
        return jnp.where(group == z, pltpu.roll(lin, lax.rem(4 * z + 2, Y), 1), packed)

    packed = lax.fori_loop(0, NZ // 2, lin_y, jnp.zeros((X, Y), F32), unroll=8)

    for t in range(n - 1):
        rim_copy(t).wait_recv()
    vh, vl = split(rrecv[...].reshape(M, Y))
    w = jnp.dot(recm[...], jnp.concatenate([vh, vl, vh], axis=0), preferred_element_type=F32)
    wsend[...] = w.reshape(n, 4 * owned, Y)

    def w_copy(t):
        who = lax.rem(i + 1 + t, n)
        return remote(wsend.at[who], wrecv.at[i], w_s.at[t], w_r.at[t], (who, j))

    for t in range(n - 1):
        w_copy(t).start()
    wrecv[i] = wsend[i]

    packed = lax.fori_loop(NZ // 2, NZ, lin_y, packed, unroll=8)
    packed = jnp.where(low, pltpu.roll(packed, Y - 2, 1), pltpu.roll(packed, 2, 1))
    for z in range(NZ):
        byr[4 * z:4 * z + 2] = by[z, 0:2, :]
        byr[4 * z + 2:4 * z + 4] = by[z, Y - 2:Y, :]
    rh, rl = split(byr[...])
    byr3[...] = jnp.concatenate([rh, rh, rl], axis=1)
    loads[3].wait()
    loads[6].wait()
    flat = jnp.concatenate([sx[z] for z in range(NZ)], axis=0)
    flat = jnp.transpose(flat, (1, 0))
    sxp[...] = flat
    sh, sl = split(flat)
    sx3[...] = jnp.concatenate([sh, sh, sl], axis=1)

    def prep_spikes(z, carry):
        spikes = pltpu.roll(sxp[...], lax.rem(Y - 4 * z, Y), 1)
        for k in range(4):
            sxb[z, k] = jnp.broadcast_to(spikes[:, k:k + 1], (X, Y))
        return carry

    lax.fori_loop(0, NZ, prep_spikes, 0, unroll=4)

    spread_z = iota((NZ, Y), 0)
    spread_l = iota((NZ, Y), 1)
    coeff = jnp.zeros((4 * m, Y), F32)
    for jj in range(4):
        off = jj - 2 if jj < 2 else jj + 2
        pick = lax.rem(4 * j + off + 4 * m, 4 * m)
        spread = jnp.where(spread_l == 4 * spread_z + jj, 1.0, 0.0)
        coeff = coeff + jnp.dot(ry[pick], spread, precision=HIGH, preferred_element_type=F32)
    ryc[...] = coeff

    for t in range(n - 1):
        w_copy(t).wait_recv()
    wh, wl = split(wrecv[...].reshape(M, Y))
    mixed = lax.dot_general(
        jnp.concatenate([wh, wl, wh], axis=1), byr3[...],
        (((1,), (1,)), ((), ())), preferred_element_type=F32)
    mixed = jnp.where((iota((M, M), 0) >> 2) == (iota((M, M), 1) >> 2), mixed, 0.0)
    mh, ml = split(mixed)
    yrims[j] = packed - jnp.dot(
        sx3[...], jnp.concatenate([mh, ml, mh], axis=0), preferred_element_type=F32)

    def g_copy(t):
        who = lax.rem(j + 1 + t, m)
        return remote(yrims.at[j], yrims.at[j], g_s.at[t], g_r.at[t], (i, who))

    for t in range(m - 1):
        g_copy(t).start()

    def fix_y(b, carry):
        for u in range(owners):
            q = b * owners + u
            fh, fl = split(wrecv[q])
            for zz in range(owned):
                z = q * owned + zz
                part = lax.dot_general(
                    jnp.concatenate([fh, fl, fh], axis=1), byc[z],
                    (((1,), (1,)), ((), ())), preferred_element_type=F32)
                value = yfull[z]
                for k in range(4):
                    value = value - sxb[z, k] * part[4 * zz + k:4 * zz + k + 1, :]
                yfull[z] = value
        return carry

    groups = n // owners
    size = NZ // groups
    stores = []
    for b in range(groups):
        fix_y(b, 0)
        store = pltpu.make_async_copy(
            yfull.at[pl.ds(b * size, size)], lin_h.at[pl.ds(b * size, size)], out_sem.at[b])
        store.start()
        stores.append(store)

    for t in range(m - 1):
        g_copy(t).wait_recv()

    total = jnp.zeros((X, Y), F32)
    klane = iota((1, Y), 1) & 3
    for g in range(m):
        field = yrims[g]
        for d in range(-3, 4):
            factor = jnp.zeros((1, Y), F32)
            for jj in range(4):
                if 0 <= jj - d < 4:
                    factor = jnp.where(klane == jj, ryc[4 * g + jj - d:4 * g + jj - d + 1, :], factor)
            total = total + factor * (field if d == 0 else pltpu.roll(field, d % Y, 1))
    total_v[...] = total
    store = pltpu.make_async_copy(total_v, total_h, out_sem.at[groups])
    store.start()
    stores.append(store)
    for copy in halo:
        copy.wait_send()
    for t in range(n - 1):
        rim_copy(t).wait_send()
        w_copy(t).wait_send()
    for t in range(m - 1):
        g_copy(t).wait_send()
    for store in stores:
        store.wait()


def finish(total_ref, spikes_ref, lin_ref, out_ref):
    size, X, Y = lin_ref.shape
    base = pl.program_id(0) * size
    for z in range(size):
        mine = pltpu.roll(total_ref[...], lax.rem(Y - 4 * (base + z), Y), 1)
        value = lin_ref[z]
        for k in range(4):
            value = value - mine[:, k:k + 1] * spikes_ref[z, k:k + 1, :]
        out_ref[z] = value


def body(conc, mobility, block_x, spike_x, reduced_x, block_y, spike_y, reduced_y):
    n, m = lax.axis_size("gx"), lax.axis_size("gy")
    NZ, X, Y = conc.shape
    owned = NZ // n
    M = 4 * NZ
    nside = 1 if m == 2 else 2
    vm = lambda *shape: pltpu.VMEM(shape, F32)
    vb = lambda *shape: pltpu.VMEM(shape, BF16)
    dma = lambda *shape: pltpu.SemaphoreType.DMA(shape)
    sxt = jnp.transpose(spike_x, (0, 2, 1))
    syt = jnp.transpose(spike_y, (0, 2, 1))
    ryt = jnp.transpose(reduced_y, (1, 2, 0))
    scratch = [
        vm(NZ, X, Y), vm(NZ, X, Y), vm(NZ, X, X), vm(NZ, 4, X), vm(owned, 4 * n, 4 * n),
        vm(NZ, Y, Y), vm(4 * m, 4 * m, NZ),
        vm(3, NZ, Y), vm(3, NZ, Y), vm(3, NZ, Y), vm(3, NZ, Y),
        vm(X + X // 2, Y), vm(nside, X + X // 2, Y), vm(2, nside, 8, Y),
        vm(2, NZ, Y), vm(2, NZ, Y), vm(X, Y), vm(X, Y), vm(X, Y),
        vb(NZ, X, 3 * X), vb(NZ, Y, 3 * Y), vm(NZ, X, Y), vm(NZ, X, Y),
        vm(n, 4 * owned, Y), vm(n, 4 * owned, Y), vb(M, 3 * M),
        vm(n, 4 * owned, Y), vm(n, 4 * owned, Y), vm(X, M), vm(m, X, Y), vm(4 * m, Y),
        vm(M, Y), vb(M, 3 * Y), vb(X, 3 * M), vm(X, Y),
        vm(NZ, X, Y), vm(NZ, X, Y), vm(NZ, X, Y), vm(NZ, 4, X, Y),
        dma(7), dma(n + 1), dma(2), dma(2), dma(nside), dma(nside), dma(2, nside), dma(2, nside),
        dma(n - 1), dma(n - 1), dma(n - 1), dma(n - 1), dma(m - 1), dma(m - 1),
    ]
    lin, total = pl.pallas_call(
        functools.partial(kernel, n, m),
        out_shape=(jax.ShapeDtypeStruct(conc.shape, F32), jax.ShapeDtypeStruct((X, Y), F32)),
        in_specs=[pl.BlockSpec(memory_space=pl.ANY)] * 7,
        out_specs=(pl.BlockSpec(memory_space=pl.ANY), pl.BlockSpec(memory_space=pl.ANY)),
        scratch_shapes=scratch,
        compiler_params=pltpu.CompilerParams(
            collective_id=0, has_side_effects=True, vmem_limit_bytes=60 * 2**20),
        cost_estimate=pl.CostEstimate(flops=10**9, bytes_accessed=8 * 2**20, transcendentals=0),
    )(conc, mobility, block_x, sxt, reduced_x, block_y, ryt)
    step = 8
    return pl.pallas_call(
        finish,
        out_shape=jax.ShapeDtypeStruct(conc.shape, F32),
        grid=(NZ // step,),
        in_specs=[
            pl.BlockSpec((X, Y), lambda g: (0, 0)),
            pl.BlockSpec((step, 4, Y), lambda g: (g, 0, 0)),
            pl.BlockSpec((step, X, Y), lambda g: (g, 0, 0)),
        ],
        out_specs=pl.BlockSpec((step, X, Y), lambda g: (g, 0, 0)),
        compiler_params=pltpu.CompilerParams(vmem_limit_bytes=60 * 2**20),
    )(total, syt, lin)


def solution(mesh):
    in_specs = (
        P(None, "gx", "gy"),
        P(None, "gx", "gy"),
        P(None, "gx", None),
        P(None, "gx", None),
        P(),
        P(None, "gy", None),
        P(None, "gy", None),
        P(),
    )
    out_specs = P(None, "gx", "gy")
    return jax.shard_map(body, mesh=mesh, in_specs=in_specs, out_specs=out_specs, check_vma=False)
```
